32 devices in a mesh: replica: 2 (over core), fsdp: 16 (over z, y, x).
Axes of the slice: x: 2, y: 2, z: 4, core: 2. Of those that a mesh axis runs over, the one named last changes fastest.
Arguments:
- layer_index: int32 [2], P('replica'), may hold values from 0 to 3
- inputs: bfloat16 [8192, 4608], P(('replica', 'fsdp')), may hold values from -6 to 6
- norm_gain: float32 [4608], replicated, may hold values from 0.1 to 1.9
- cotangent: bfloat16 [8192, 1024], P(('replica', 'fsdp')), may hold values from -6 to 6
- local_fragment: bfloat16 [2, 4, 4608, 1024], P('replica', None, 'fsdp'), may hold values from -6 to 6
- global_fragment: float32 [4, 4608, 1024], P(None, 'fsdp'), may hold values from -6 to 6
- momentum: float32 [4, 4608, 1024], P(None, 'fsdp'), may hold values from -4 to 4
Outputs:
- keys_block: bfloat16 [8192, 1024], P(('replica', 'fsdp'))
- weight_grad: float32 [2, 4608, 1024], P('replica', 'fsdp')
- new_global: float32 [4, 4608, 1024], P(None, 'fsdp')
- new_momentum: float32 [4, 4608, 1024], P(None, 'fsdp')
The draws below stay inside these ranges and needn't reach their ends.
Inputs may be any that keep to these rules, and one draw needn't show every extreme that they name: `layer_index`: a layer of the fragment for each replica.
All inputs are finite; a program needn't handle non-finite values.
Results may differ from the reference program's by a relative error of at most 0.0049.
Values may be sent and summed in bfloat16 or wider, within the bound.
A program may use at most 128 MiB of HBM per device.

```python
import jax
import jax.numpy as jnp
from jax import lax

D = 4608
KV = 1024
FRAG = 4
TOKENS = 4096
ALL_TOKENS = 8192
N_REPLICA = 2


def spiked(result, rng, source, target, parts, factor):
    def block_of(position):
        return (jnp.arange(result.shape[position]) // (result.shape[position] // parts)).reshape((-1,) + (1,) * (result.ndim - 1 - position))

    near = jax.random.permutation(rng, parts)[block_of(target)]
    other_side = (block_of(target) + parts // 2) % parts
    return jnp.where((block_of(source) == near) | (block_of(source) == other_side), factor * result, result)


def steps_of(own_key, dims, shards, low, high):
    def one(dim, parts):
        steps = jax.random.uniform(jax.random.fold_in(jax.random.fold_in(own_key, 6), dim), (parts,), jnp.float32, low / len(shards), high / len(shards))
        return jnp.repeat(jnp.exp(steps), dims[dim] // parts).reshape((-1,) + (1,) * (len(dims) - dim - 1))

    level = one(*shards[0])
    for cut in shards[1:]:
        level = level * one(*cut)
    return level


def bell_draw(rng, extent, spread, bound, shards=(), held_as=jnp.bfloat16):
    result = jax.random.normal(rng, extent, jnp.float32) * spread
    if len(shards) > 0:
        result = steps_of(rng, extent, shards, -0.22, 0.18) * result
    return jnp.clip(result, min=-bound, max=bound).astype(held_as)


def gaussian_with(own_key, dims, width, reach, cuts, heavy, kind=jnp.bfloat16):
    entries = width * jax.random.normal(own_key, dims, jnp.float32)
    if cuts:
        entries = entries * steps_of(own_key, dims, cuts, -0.22, 0.18)
    return jnp.clip(spiked(entries, jax.random.fold_in(own_key, 3), *heavy), -reach, reach).astype(kind)


def setup_inputs(seed: int = 0) -> dict:
    keys = jax.random.split(jax.random.key(seed), 8)
    layer_index = jax.random.randint(keys[0], (N_REPLICA,), 0, FRAG).astype(jnp.int32)
    inputs = gaussian_with(keys[1], (ALL_TOKENS, D), 1.0, 6.0, ((0, 32),), (0, 1, 32, 2.75))
    norm_gain = jnp.clip(1.0 + 0.18 * jax.random.normal(keys[2], (D,), jnp.float32), 0.1, 1.9)
    cotangent = bell_draw(keys[3], (ALL_TOKENS, KV), 1.0, 6.0, ((0, 32),))
    local_fragment = bell_draw(keys[4], (N_REPLICA, FRAG, D, KV), 1.0, 6.0, ((0, 2), (2, 16)))
    global_fragment = bell_draw(keys[5], (FRAG, D, KV), 1.0, 6.0, ((1, 16),), jnp.float32)
    momentum = bell_draw(keys[6], (FRAG, D, KV), 0.5, 4.0, ((1, 16),), jnp.float32)
    return {"layer_index": layer_index, "inputs": inputs, "norm_gain": norm_gain, "cotangent": cotangent, "local_fragment": local_fragment, "global_fragment": global_fragment, "momentum": momentum}


def reference(layer_index, inputs, norm_gain, cotangent, local_fragment, global_fragment, momentum):
    scale_factor = float(D) ** (-0.5)
    token_blocks = inputs.reshape(N_REPLICA, TOKENS, D)
    cot_blocks = cotangent.reshape(N_REPLICA, TOKENS, KV)

    def one_replica(packed):
        chosen, tokens_here, cot_here, fragment_here = packed
        values = tokens_here.astype(jnp.float32)
        stats = lax.optimization_barrier(jnp.mean(values * values, axis=1, keepdims=True))
        normed = (values * lax.rsqrt(stats + 1e-06) * norm_gain[None, :]).astype(jnp.bfloat16)
        layer = lax.dynamic_index_in_dim(fragment_here, chosen.astype(jnp.int32), 0, keepdims=False)
        keys_here = (jnp.dot(normed, layer, preferred_element_type=jnp.float32) * scale_factor).astype(jnp.bfloat16)
        grad_here = jnp.dot(normed.T, cot_here, preferred_element_type=jnp.float32) * scale_factor
        return (keys_here, grad_here)
    keys_all, weight_grad = lax.map(one_replica, (layer_index, token_blocks, cot_blocks, local_fragment))
    keys_block = keys_all.reshape(ALL_TOKENS, KV)
    delta = global_fragment[None] - local_fragment.astype(jnp.float32)
    average = lax.optimization_barrier(jnp.sum(delta, axis=0)) / N_REPLICA
    new_momentum = 0.9 * momentum + average
    new_global = global_fragment - 0.7 * (average + 0.9 * new_momentum)
    return (keys_block, weight_grad, new_global, new_momentum)
```

```python
import functools

import jax
import jax.numpy as jnp
from jax import lax
from jax.experimental import pallas as pl
from jax.experimental.pallas import tpu as pltpu
from jax.sharding import PartitionSpec as P

INNER = 4
LANES = 128


def kernel(
    R, G, O, x_ref, gain_ref, cot_ref, w_ref, frag_in, keys_ref, grad_ref, frag_out,
    inv, nt, a, cots, ws, part, out_buf, in_buf, key_own, key_out, key_in,
    local_sem, frag_s, frag_r, cot_s, cot_r, w_s, w_r, norm_s, norm_r, key_s, key_r, sum_s, sum_r,
):
    T, D = x_ref.shape
    KV = cot_ref.shape[1]
    F = D // (G * O)
    scale = float(D) ** (-0.5)
    r = lax.axis_index("replica")
    i = lax.axis_index("fsdp")
    z, c = i // G, i % G

    def at(replica, outer, inner):
        return {"replica": replica, "fsdp": outer * G + inner}

    def remote(src, dst, send, recv, target):
        return pltpu.make_async_remote_copy(
            src_ref=src, dst_ref=dst, send_sem=send, recv_sem=recv,
            device_id=target, device_id_type=pl.DeviceIdType.MESH,
        )

    def rows(block, size):
        return pl.ds(pl.multiple_of(block * size, size), size)

    barrier = pltpu.get_barrier_semaphore()

    def greet(target):
        pl.semaphore_signal(barrier, inc=1, device_id=target, device_id_type=pl.DeviceIdType.MESH)

    for k in range(1, G):
        greet(at(r, z, (c + k) % G))
    for k in range(1, R):
        greet(at((r + k) % R, z, c))
    has_left, has_right = z > 0, z < O - 1

    @pl.when(has_left)
    def _():
        greet(at(r, z - 1, c))

    @pl.when(has_right)
    def _():
        greet(at(r, z + 1, c))

    pl.semaphore_wait(barrier, G - 1 + R - 1 + jnp.where(has_left, 1, 0) + jnp.where(has_right, 1, 0))

    def cot_copy(k):
        return remote(cot_ref, cots.at[rows(c, T)], cot_s.at[k], cot_r.at[k], at(r, z, (c + k) % G))

    def frag_copy(k):
        return remote(frag_in, frag_out.at[r], frag_s.at[k], frag_r.at[k], at((r + k) % R, z, c))

    def w_copy(side, hop):
        block = z - (hop - 1) if side == 0 else z + (hop - 1)
        where = ws.at[rows(block, F)]
        return remote(
            w_ref if hop == 1 else where, where, w_s.at[side, hop], w_r.at[side, hop],
            at(r, z + 1 if side == 0 else z - 1, c),
        )

    def w_sends(side, hop):
        if side == 0:
            return jnp.logical_and(z >= hop - 1, z < O - 1)
        return jnp.logical_and(z + hop - 1 <= O - 1, z > 0)

    def w_comes(side, hop):
        return z >= hop if side == 0 else z + hop <= O - 1

    def w_start(hop):
        for side in range(2):
            @pl.when(w_sends(side, hop))
            def _(side=side):
                w_copy(side, hop).start()

    def w_wait(hop):
        for side in range(2):
            @pl.when(w_comes(side, hop))
            def _(side=side):
                block = z - hop if side == 0 else z + hop
                where = ws.at[rows(block, F)]
                remote(where, where, w_s.at[side, hop], w_r.at[side, hop], at(r, z, (c + 1) % G)).wait_recv()

    for k in range(1, G):
        cot_copy(k).start()
    w_start(1)
    for k in range(1, R):
        frag_copy(k).start()
    mine = [
        pltpu.make_async_copy(cot_ref, cots.at[rows(c, T)], local_sem.at[0]),
        pltpu.make_async_copy(w_ref, ws.at[rows(z, F)], local_sem.at[1]),
        pltpu.make_async_copy(frag_in, frag_out.at[r], local_sem.at[2]),
    ]
    for copy in mine:
        copy.start()

    step = 16

    @pl.loop(0, T // step)
    def _(t):
        here = pl.ds(pl.multiple_of(t * step, step), step)
        values = x_ref[here, :].astype(jnp.float32)
        stats = jnp.mean(values * values, axis=1, keepdims=True)
        inv[here, :] = jnp.broadcast_to(lax.rsqrt(stats + 1e-06), (step, LANES))

    def transpose_chunks(start, count):
        @pl.loop(0, count)
        def _(j):
            here = pl.ds(pl.multiple_of(start + j * LANES, LANES), LANES)
            normed = x_ref[:, here].astype(jnp.float32) * inv[...] * gain_ref[:, here]
            nt[here, :] = normed.T.astype(jnp.bfloat16)

    def order(k):
        far = O - 1 - k // 2 if k % 2 == 0 else k // 2
        return jnp.where(z < O // 2, far, O - 1 - far)

    def norm_copy(d, k):
        peer = (c + k) % G
        return remote(
            nt.at[rows(d * G + peer, F)],
            a.at[rows(d, F), rows(c, T)],
            norm_s.at[d, k], norm_r.at[d, k], at(r, z, peer),
        )

    whole = (G * F) % LANES != 0
    if whole:
        transpose_chunks(0, D // LANES)
    for n in range(O):
        d = order(n)
        if not whole:
            transpose_chunks(d * (G * F), G * F // LANES)
        for k in range(1, G):
            norm_copy(d, k).start()
        a[rows(d, F), rows(c, T)] = nt[rows(d * G + c, F), :]

    def sum_copy(d):
        side = jnp.where(z < d, 0, 1)
        return remote(
            out_buf.at[d], in_buf.at[side, d], sum_s.at[d], sum_r.at[side, d],
            at(r, jnp.where(z < d, z + 1, z - 1), c),
        )

    def sum_wait(side, d):
        where = in_buf.at[side, d]
        remote(where, where, sum_s.at[d], sum_r.at[side, d], at(r, z, (c + 1) % G)).wait_recv()

    tile = min(512, KV)
    for n in range(O):
        d = order(n)
        if n + 1 < O:
            w_wait(n + 1)
            if n + 2 < O:
                w_start(n + 2)
        if n == 0:
            for copy in mine:
                copy.wait()
            for k in range(1, G):
                cot_copy(k).wait_recv()
        for k in range(1, G):
            norm_copy(d, k).wait_recv()
        for m in range(KV // tile):
            cols = pl.ds(m * tile, tile)
            part[d, :, cols] = jnp.dot(a[rows(d, F), :], cots[:, cols], preferred_element_type=jnp.float32)
        first = jnp.logical_or(jnp.logical_and(z == 0, d > 0), jnp.logical_and(z == O - 1, d < O - 1))

        @pl.when(first)
        def _(d=d):
            out_buf[d] = part[d].astype(jnp.bfloat16)
            sum_copy(d).start()

    def key_copy(k):
        return remote(key_out.at[k], key_in.at[k], key_s.at[k], key_r.at[k], at(r, z, (c + k) % G))

    for k in list(range(1, G)) + [0]:
        tokens = rows((c + k) % G, T)
        for m in range(KV // tile):
            cols = pl.ds(m * tile, tile)
            term = lax.dot_general(
                a[:, tokens], ws[:, cols], (((0,), (0,)), ((), ())), preferred_element_type=jnp.float32
            )
            if k:
                key_out[k, :, cols] = term.astype(jnp.bfloat16)
            else:
                key_own[:, cols] = term
        if k:
            key_copy(k).start()

    for n in range(O):
        d = order(n)
        between = jnp.logical_and(d != z, jnp.logical_and(z > 0, z < O - 1))

        @pl.when(between)
        def _(d=d):
            side = jnp.where(z < d, 0, 1)
            sum_wait(side, d)
            out_buf[d] = (part[d] + in_buf[side, d].astype(jnp.float32)).astype(jnp.bfloat16)
            sum_copy(d).start()

    grad_ref[...] = part[z]

    @pl.when(has_left)
    def _():
        sum_wait(0, z)
        grad_ref[...] += in_buf[0, z].astype(jnp.float32)

    @pl.when(has_right)
    def _():
        sum_wait(1, z)
        grad_ref[...] += in_buf[1, z].astype(jnp.float32)

    grad_ref[...] = grad_ref[...] * scale

    for k in range(1, G):
        key_copy(k).wait_recv()
    total = key_own[...]
    for k in range(1, G):
        total = total + key_in[k].astype(jnp.float32)
    keys_ref[...] = (total * scale).astype(jnp.bfloat16)

    for k in range(1, R):
        frag_copy(k).wait()
    for k in range(1, G):
        cot_copy(k).wait_send()
        key_copy(k).wait_send()
    for d in range(O):
        for k in range(1, G):
            norm_copy(d, k).wait_send()

        @pl.when(z != d)
        def _(d=d):
            sum_copy(d).wait_send()
    for hop in range(1, O):
        for side in range(2):
            @pl.when(w_sends(side, hop))
            def _(side=side, hop=hop):
                w_copy(side, hop).wait_send()


def body(layer_index, inputs, norm_gain, cotangent, local_fragment, global_fragment, momentum):
    R, S = lax.axis_size("replica"), lax.axis_size("fsdp")
    G = INNER
    O = S // G
    T, D = inputs.shape
    KV = cotangent.shape[1]
    F = D // S
    own = local_fragment[0]
    layer = lax.dynamic_index_in_dim(own, layer_index[0], 0, keepdims=False)
    bf16, f32 = jnp.bfloat16, jnp.float32
    vmem, anywhere = pl.BlockSpec(memory_space=pltpu.VMEM), pl.BlockSpec(memory_space=pl.ANY)
    dma = pltpu.SemaphoreType.DMA
    keys_block, grad, fragments = pl.pallas_call(
        functools.partial(kernel, R, G, O),
        out_shape=(
            jax.ShapeDtypeStruct((T, KV), bf16),
            jax.ShapeDtypeStruct((F, KV), f32),
            jax.ShapeDtypeStruct((R,) + own.shape, bf16),
        ),
        in_specs=[vmem, vmem, anywhere, anywhere, anywhere],
        out_specs=(vmem, vmem, anywhere),
        scratch_shapes=[
            pltpu.VMEM((T, LANES), f32),
            pltpu.VMEM((D, T), bf16),
            pltpu.VMEM((O * F, G * T), bf16),
            pltpu.VMEM((G * T, KV), bf16),
            pltpu.VMEM((O * F, KV), bf16),
            pltpu.VMEM((O, F, KV), f32),
            pltpu.VMEM((O, F, KV), bf16),
            pltpu.VMEM((2, O, F, KV), bf16),
            pltpu.VMEM((T, KV), f32),
            pltpu.VMEM((G, T, KV), bf16),
            pltpu.VMEM((G, T, KV), bf16),
            dma((3,)), dma((R,)), dma((R,)), dma((G,)), dma((G,)),
            dma((2, O)), dma((2, O)), dma((O, G)), dma((O, G)),
            dma((G,)), dma((G,)), dma((O,)), dma((2, O)),
        ],
        compiler_params=pltpu.CompilerParams(
            collective_id=0, has_side_effects=True, vmem_limit_bytes=56 * 1024 * 1024
        ),
        cost_estimate=pl.CostEstimate(flops=4 * T * D * KV, bytes_accessed=16 * 1024 * 1024, transcendentals=T),
    )(inputs, norm_gain[None, :], cotangent, layer, own)
    weight_grad = grad[None]
    total = global_fragment - fragments[0].astype(f32)
    for k in range(1, R):
        total = total + (global_fragment - fragments[k].astype(f32))
    average = total / R
    new_momentum = 0.9 * momentum + average
    new_global = global_fragment - 0.7 * (average + 0.9 * new_momentum)
    return (keys_block, weight_grad, new_global, new_momentum)


def solution(mesh):
    placed = (
        P("replica"),
        P(("replica", "fsdp"), None),
        P(),
        P(("replica", "fsdp"), None),
        P("replica", None, "fsdp", None),
        P(None, "fsdp", None),
        P(None, "fsdp", None),
    )
    return jax.shard_map(
        body,
        mesh=mesh,
        in_specs=placed,
        out_specs=(
            P(("replica", "fsdp"), None),
            P("replica", "fsdp", None),
            P(None, "fsdp", None),
            P(None, "fsdp", None),
        ),
        check_vma=False,
    )
```

```python
import functools

import jax
import jax.numpy as jnp
from jax import lax
from jax.experimental import pallas as pl
from jax.experimental.pallas import tpu as pltpu
from jax.sharding import PartitionSpec as P

INNER = 4
LANES = 128


def kernel(
    R, G, O, pick_ref, x_ref, gain_ref, cot_ref, frag_in, keys_ref, grad_ref, frag_out,
    inv, nt, a, cots, ws, part, out_buf, in_buf, key_own, key_add, key_out, key_in,
    local_sem, frag_s, frag_r, cot_s, cot_r, w_s, w_r, norm_s, norm_r, key_s, key_r, sum_s, sum_r,
):
    T, D = x_ref.shape
    KV = cot_ref.shape[1]
    F = D // (G * O)
    scale = float(D) ** (-0.5)
    r = lax.axis_index("replica")
    i = lax.axis_index("fsdp")
    z, c = i // G, i % G
    cx, cy = c % 2, c // 2
    plane = [c, cy * 2 + 1 - cx, (1 - cy) * 2 + cx, 3 - c]

    def at(replica, outer, inner):
        return {"replica": replica, "fsdp": outer * G + inner}

    def remote(src, dst, send, recv, target):
        return pltpu.make_async_remote_copy(
            src_ref=src, dst_ref=dst, send_sem=send, recv_sem=recv,
            device_id=target, device_id_type=pl.DeviceIdType.MESH,
        )

    def rows(block, size):
        return pl.ds(pl.multiple_of(block * size, size), size)

    barrier = pltpu.get_barrier_semaphore()

    def greet(target):
        pl.semaphore_signal(barrier, inc=1, device_id=target, device_id_type=pl.DeviceIdType.MESH)

    for k in range(1, G):
        greet(at(r, z, plane[k]))
    for k in range(1, R):
        greet(at((r + k) % R, z, c))
    has_left, has_right = z > 0, z < O - 1

    @pl.when(has_left)
    def _():
        greet(at(r, z - 1, c))

    @pl.when(has_right)
    def _():
        greet(at(r, z + 1, c))

    pl.semaphore_wait(barrier, G - 1 + R - 1 + jnp.where(has_left, 1, 0) + jnp.where(has_right, 1, 0))

    half = T // 2

    def cot_copy(k):
        return remote(cot_ref, cots.at[rows(c, T)], cot_s.at[k], cot_r.at[k], at(r, z, plane[k]))

    def cot_pass(k):
        where = cots.at[pl.ds(pl.multiple_of(plane[k] * T + (k - 1) * half, half), half)]
        return remote(where, where, cot_s.at[2 + k], cot_r.at[2 + k], at(r, z, plane[3 - k]))

    def cot_passed(k):
        where = cots.at[pl.ds(pl.multiple_of(plane[3] * T + (2 - k) * half, half), half)]
        return remote(where, where, cot_s.at[5 - k], cot_r.at[5 - k], at(r, z, plane[k]))

    def frag_copy(k):
        return remote(frag_in, frag_out.at[r], frag_s.at[k], frag_r.at[k], at((r + k) % R, z, c))

    def w_copy(side, hop):
        block = z - (hop - 1) if side == 0 else z + (hop - 1)
        where = ws.at[rows(block, F)]
        return remote(
            where, where, w_s.at[side, hop], w_r.at[side, hop],
            at(r, z + 1 if side == 0 else z - 1, c),
        )

    def w_sends(side, hop):
        if side == 0:
            return jnp.logical_and(z >= hop - 1, z < O - 1)
        return jnp.logical_and(z + hop - 1 <= O - 1, z > 0)

    def w_comes(side, hop):
        return z >= hop if side == 0 else z + hop <= O - 1

    def w_start(hop):
        for side in range(2):
            @pl.when(w_sends(side, hop))
            def _(side=side):
                w_copy(side, hop).start()

    def w_wait(hop):
        for side in range(2):
            @pl.when(w_comes(side, hop))
            def _(side=side):
                block = z - hop if side == 0 else z + hop
                where = ws.at[rows(block, F)]
                remote(where, where, w_s.at[side, hop], w_r.at[side, hop], at(r, z, plane[1])).wait_recv()

    for k in (1, 2):
        cot_copy(k).start()
    ws[rows(z, F), :] = frag_in[pick_ref[0]]
    w_start(1)
    mine = [
        pltpu.make_async_copy(cot_ref, cots.at[rows(c, T)], local_sem.at[0]),
        pltpu.make_async_copy(frag_in, frag_out.at[r], local_sem.at[1]),
    ]
    for copy in mine:
        copy.start()

    step = 16

    @pl.loop(0, T // step)
    def _(t):
        here = pl.ds(pl.multiple_of(t * step, step), step)
        values = x_ref[here, :].astype(jnp.float32)
        stats = jnp.mean(values * values, axis=1, keepdims=True)
        inv[here, :] = jnp.broadcast_to(lax.rsqrt(stats + 1e-06), (step, LANES))

    def transpose_chunks(start, count):
        @pl.loop(0, count)
        def _(j):
            here = pl.ds(pl.multiple_of(start + j * LANES, LANES), LANES)
            normed = x_ref[:, here].astype(jnp.float32) * inv[...] * gain_ref[:, here]
            nt[here, :] = normed.T.astype(jnp.bfloat16)

    def order(k):
        far = O - 1 - k // 2 if k % 2 == 0 else k // 2
        return jnp.where(z < O // 2, far, O - 1 - far)

    def norm_copy(d, k):
        peer = plane[k]
        return remote(
            nt.at[rows(d * G + peer, F)],
            a.at[rows(d, F), rows(c, T)],
            norm_s.at[d, k], norm_r.at[d, k], at(r, z, peer),
        )

    whole = (G * F) % LANES != 0
    if whole:
        transpose_chunks(0, D // LANES)
    for n in range(O):
        d = order(n)
        if not whole:
            transpose_chunks(d * (G * F), G * F // LANES)
        for k in range(1, G):
            norm_copy(d, k).start()
        a[rows(d, F), rows(c, T)] = nt[rows(d * G + c, F), :]
        if n == min(1, O - 1):
            for k in (1, 2):
                cot_copy(k).wait_recv()
                cot_pass(k).start()
    for k in range(1, R):
        frag_copy(k).start()

    def sum_copy(d):
        side = jnp.where(z < d, 0, 1)
        return remote(
            out_buf.at[d], in_buf.at[side, d], sum_s.at[d], sum_r.at[side, d],
            at(r, jnp.where(z < d, z + 1, z - 1), c),
        )

    def sum_wait(side, d):
        where = in_buf.at[side, d]
        remote(where, where, sum_s.at[d], sum_r.at[side, d], at(r, z, plane[1])).wait_recv()

    def pass_on(d):
        between = jnp.logical_and(d != z, jnp.logical_and(z > 0, z < O - 1))

        @pl.when(between)
        def _():
            side = jnp.where(z < d, 0, 1)
            sum_wait(side, d)
            out_buf[d] = (part[d] + in_buf[side, d].astype(jnp.float32)).astype(jnp.bfloat16)
            sum_copy(d).start()

    tile = min(512, KV)
    for n in range(O):
        d = order(n)
        if n + 1 < O:
            w_wait(n + 1)
            if n + 2 < O:
                w_start(n + 2)
        if n == 0:
            for copy in mine:
                copy.wait()
            for k in (1, 2):
                cot_passed(k).wait_recv()
        for k in range(1, G):
            norm_copy(d, k).wait_recv()
        for m in range(KV // tile):
            cols = pl.ds(m * tile, tile)
            part[d, :, cols] = jnp.dot(a[rows(d, F), :], cots[:, cols], preferred_element_type=jnp.float32)
        first = jnp.logical_or(jnp.logical_and(z == 0, d > 0), jnp.logical_and(z == O - 1, d < O - 1))

        @pl.when(first)
        def _(d=d):
            out_buf[d] = part[d].astype(jnp.bfloat16)
            sum_copy(d).start()

        if n == O - 2:
            pass_on(order(0))

    top, bottom = pl.ds(0, half), pl.ds(half, half)

    def key_term(k, put):
        tokens = rows(plane[k], T)
        for m in range(KV // tile):
            cols = pl.ds(m * tile, tile)
            put(cols, lax.dot_general(
                a[:, tokens], ws[:, cols], (((0,), (0,)), ((), ())), preferred_element_type=jnp.float32
            ))

    def key_copy(k, part_of, slot, target):
        return remote(
            key_out.at[k, part_of], key_in.at[k, part_of], key_s.at[slot], key_r.at[slot], at(r, z, target)
        )

    across = [key_copy(3, top, 0, plane[1]), key_copy(3, bottom, 1, plane[2])]
    plain = [key_copy(1, top, 2, plane[1]), key_copy(2, bottom, 3, plane[2])]
    summed = [key_copy(1, bottom, 4, plane[1]), key_copy(2, top, 5, plane[2])]

    def put_across(cols, term):
        key_out[3, :, cols] = term.astype(jnp.bfloat16)

    key_term(3, put_across)
    for copy in across:
        copy.start()

    def put_x(cols, term):
        key_out[1, top, cols] = term[:half].astype(jnp.bfloat16)
        key_add[0, :, cols] = term[half:]

    key_term(1, put_x)
    plain[0].start()

    def put_y(cols, term):
        key_out[2, bottom, cols] = term[half:].astype(jnp.bfloat16)
        key_add[1, :, cols] = term[:half]

    key_term(2, put_y)
    plain[1].start()

    def put_own(cols, term):
        key_own[:, cols] = term

    key_term(0, put_own)
    across[1].wait_recv()
    key_out[1, bottom, :] = (key_add[0] + key_in[3, bottom, :].astype(jnp.float32)).astype(jnp.bfloat16)
    summed[0].start()
    across[0].wait_recv()
    key_out[2, top, :] = (key_add[1] + key_in[3, top, :].astype(jnp.float32)).astype(jnp.bfloat16)
    summed[1].start()

    for n in range(1, O):
        pass_on(order(n))

    grad_ref[...] = part[z]

    @pl.when(has_left)
    def _():
        sum_wait(0, z)
        grad_ref[...] += in_buf[0, z].astype(jnp.float32)

    @pl.when(has_right)
    def _():
        sum_wait(1, z)
        grad_ref[...] += in_buf[1, z].astype(jnp.float32)

    grad_ref[...] = grad_ref[...] * scale

    for copy in plain + summed:
        copy.wait_recv()
    total = key_own[...] + key_in[1].astype(jnp.float32) + key_in[2].astype(jnp.float32)
    keys_ref[...] = (total * scale).astype(jnp.bfloat16)

    for k in range(1, R):
        frag_copy(k).wait()
    for copy in across + plain + summed:
        copy.wait_send()
    for k in (1, 2):
        cot_copy(k).wait_send()
        cot_pass(k).wait_send()
    for d in range(O):
        for k in range(1, G):
            norm_copy(d, k).wait_send()

        @pl.when(z != d)
        def _(d=d):
            sum_copy(d).wait_send()
    for hop in range(1, O):
        for side in range(2):
            @pl.when(w_sends(side, hop))
            def _(side=side, hop=hop):
                w_copy(side, hop).wait_send()


def body(layer_index, inputs, norm_gain, cotangent, local_fragment, global_fragment, momentum):
    R, S = lax.axis_size("replica"), lax.axis_size("fsdp")
    G = INNER
    O = S // G
    T, D = inputs.shape
    KV = cotangent.shape[1]
    F = D // S
    own = local_fragment[0]
    bf16, f32 = jnp.bfloat16, jnp.float32
    vmem, anywhere = pl.BlockSpec(memory_space=pltpu.VMEM), pl.BlockSpec(memory_space=pl.ANY)
    dma = pltpu.SemaphoreType.DMA
    keys_block, grad, fragments = pl.pallas_call(
        functools.partial(kernel, R, G, O),
        out_shape=(
            jax.ShapeDtypeStruct((T, KV), bf16),
            jax.ShapeDtypeStruct((F, KV), f32),
            jax.ShapeDtypeStruct((R,) + own.shape, bf16),
        ),
        in_specs=[pl.BlockSpec(memory_space=pltpu.SMEM), vmem, vmem, vmem, vmem],
        out_specs=(vmem, vmem, anywhere),
        scratch_shapes=[
            pltpu.VMEM((T, LANES), f32),
            pltpu.VMEM((D, T), bf16),
            pltpu.VMEM((O * F, G * T), bf16),
            pltpu.VMEM((G * T, KV), bf16),
            pltpu.VMEM((O * F, KV), bf16),
            pltpu.VMEM((O, F, KV), f32),
            pltpu.VMEM((O, F, KV), bf16),
            pltpu.VMEM((2, O, F, KV), bf16),
            pltpu.VMEM((T, KV), f32),
            pltpu.VMEM((2, T // 2, KV), f32),
            pltpu.VMEM((G, T, KV), bf16),
            pltpu.VMEM((G, T, KV), bf16),
            dma((2,)), dma((R,)), dma((R,)), dma((5,)), dma((5,)),
            dma((2, O)), dma((2, O)), dma((O, G)), dma((O, G)),
            dma((6,)), dma((6,)), dma((O,)), dma((2, O)),
        ],
        compiler_params=pltpu.CompilerParams(
            collective_id=0, has_side_effects=True, vmem_limit_bytes=56 * 1024 * 1024
        ),
        cost_estimate=pl.CostEstimate(flops=4 * T * D * KV, bytes_accessed=16 * 1024 * 1024, transcendentals=T),
    )(layer_index, inputs, norm_gain[None, :], cotangent, own)
    weight_grad = grad[None]
    total = global_fragment - fragments[0].astype(f32)
    for k in range(1, R):
        total = total + (global_fragment - fragments[k].astype(f32))
    average = total / R
    new_momentum = 0.9 * momentum + average
    new_global = global_fragment - 0.7 * (average + 0.9 * new_momentum)
    return (keys_block, weight_grad, new_global, new_momentum)


def solution(mesh):
    placed = (
        P("replica"),
        P(("replica", "fsdp"), None),
        P(),
        P(("replica", "fsdp"), None),
        P("replica", None, "fsdp", None),
        P(None, "fsdp", None),
        P(None, "fsdp", None),
    )
    return jax.shard_map(
        body,
        mesh=mesh,
        in_specs=placed,
        out_specs=(
            P(("replica", "fsdp"), None),
            P("replica", "fsdp", None),
            P(None, "fsdp", None),
            P(None, "fsdp", None),
        ),
        check_vma=False,
    )
```

```python
import functools

import jax
import jax.numpy as jnp
from jax import lax
from jax.experimental import pallas as pl
from jax.experimental.pallas import tpu as pltpu
from jax.sharding import PartitionSpec as P

INNER = 4
LANES = 128


def kernel(
    R, G, O, pick_ref, x_hbm, gain_ref, cot_ref, frag_hbm, keys_ref, grad_ref, frag_out,
    x_ref, frag_in, inv, nt, a, cots, ws, part, out_buf, in_buf, key_own, key_add, key_out, key_in,
    local_sem, frag_s, frag_r, cot_s, cot_r, w_s, w_r, norm_s, norm_r, key_s, key_r, sum_s, sum_r,
):
    T, D = x_ref.shape
    KV = cot_ref.shape[1]
    F = D // (G * O)
    scale = float(D) ** (-0.5)
    r = lax.axis_index("replica")
    i = lax.axis_index("fsdp")
    z, c = i // G, i % G
    cx, cy = c % 2, c // 2
    plane = [c, cy * 2 + 1 - cx, (1 - cy) * 2 + cx, 3 - c]

    def at(replica, outer, inner):
        return {"replica": replica, "fsdp": outer * G + inner}

    def remote(src, dst, send, recv, target):
        return pltpu.make_async_remote_copy(
            src_ref=src, dst_ref=dst, send_sem=send, recv_sem=recv,
            device_id=target, device_id_type=pl.DeviceIdType.MESH,
        )

    def rows(block, size):
        return pl.ds(pl.multiple_of(block * size, size), size)

    load_x = pltpu.make_async_copy(x_hbm, x_ref, local_sem.at[2])
    load_frag = pltpu.make_async_copy(frag_hbm, frag_in, local_sem.at[3])
    load_frag.start()
    load_x.start()

    barrier = pltpu.get_barrier_semaphore()

    def greet(target):
        pl.semaphore_signal(barrier, inc=1, device_id=target, device_id_type=pl.DeviceIdType.MESH)

    for k in range(1, G):
        greet(at(r, z, plane[k]))
    for k in range(1, R):
        greet(at((r + k) % R, z, c))
    has_left, has_right = z > 0, z < O - 1

    @pl.when(has_left)
    def _():
        greet(at(r, z - 1, c))

    @pl.when(has_right)
    def _():
        greet(at(r, z + 1, c))

    pl.semaphore_wait(barrier, G - 1 + R - 1 + jnp.where(has_left, 1, 0) + jnp.where(has_right, 1, 0))

    half = T // 2

    def cot_copy(k):
        return remote(cot_ref, cots.at[rows(c, T)], cot_s.at[k], cot_r.at[k], at(r, z, plane[k]))

    def cot_pass(k):
        where = cots.at[pl.ds(pl.multiple_of(plane[k] * T + (k - 1) * half, half), half)]
        return remote(where, where, cot_s.at[2 + k], cot_r.at[2 + k], at(r, z, plane[3 - k]))

    def cot_passed(k):
        where = cots.at[pl.ds(pl.multiple_of(plane[3] * T + (2 - k) * half, half), half)]
        return remote(where, where, cot_s.at[5 - k], cot_r.at[5 - k], at(r, z, plane[k]))

    def frag_copy(k):
        return remote(frag_in, frag_out.at[r], frag_s.at[k], frag_r.at[k], at((r + k) % R, z, c))

    def w_copy(side, hop):
        block = z - (hop - 1) if side == 0 else z + (hop - 1)
        where = ws.at[rows(block, F)]
        return remote(
            where, where, w_s.at[side, hop], w_r.at[side, hop],
            at(r, z + 1 if side == 0 else z - 1, c),
        )

    def w_sends(side, hop):
        if side == 0:
            return jnp.logical_and(z >= hop - 1, z < O - 1)
        return jnp.logical_and(z + hop - 1 <= O - 1, z > 0)

    def w_comes(side, hop):
        return z >= hop if side == 0 else z + hop <= O - 1

    def w_start(hop):
        for side in range(2):
            @pl.when(w_sends(side, hop))
            def _(side=side):
                w_copy(side, hop).start()

    def w_wait(hop):
        for side in range(2):
            @pl.when(w_comes(side, hop))
            def _(side=side):
                block = z - hop if side == 0 else z + hop
                where = ws.at[rows(block, F)]
                remote(where, where, w_s.at[side, hop], w_r.at[side, hop], at(r, z, plane[1])).wait_recv()

    for k in (1, 2):
        cot_copy(k).start()
    load_frag.wait()
    ws[rows(z, F), :] = frag_in[pick_ref[0]]
    w_start(1)
    mine = [
        pltpu.make_async_copy(cot_ref, cots.at[rows(c, T)], local_sem.at[0]),
        pltpu.make_async_copy(frag_in, frag_out.at[r], local_sem.at[1]),
    ]
    for copy in mine:
        copy.start()

    load_x.wait()
    step = 16

    @pl.loop(0, T // step)
    def _(t):
        here = pl.ds(pl.multiple_of(t * step, step), step)
        values = x_ref[here, :].astype(jnp.float32)
        stats = jnp.mean(values * values, axis=1, keepdims=True)
        inv[here, :] = jnp.broadcast_to(lax.rsqrt(stats + 1e-06), (step, LANES))

    def transpose_chunks(start, count):
        @pl.loop(0, count)
        def _(j):
            here = pl.ds(pl.multiple_of(start + j * LANES, LANES), LANES)
            normed = x_ref[:, here].astype(jnp.float32) * inv[...] * gain_ref[here][None, :]
            nt[here, :] = normed.T.astype(jnp.bfloat16)

    def order(k):
        far = O - 1 - k // 2 if k % 2 == 0 else k // 2
        return jnp.where(z < O // 2, far, O - 1 - far)

    def norm_copy(d, k):
        peer = plane[k]
        return remote(
            nt.at[rows(d * G + peer, F)],
            a.at[rows(d, F), rows(c, T)],
            norm_s.at[d, k], norm_r.at[d, k], at(r, z, peer),
        )

    whole = (G * F) % LANES != 0
    if whole:
        transpose_chunks(0, D // LANES)
    for n in range(O):
        d = order(n)
        if not whole:
            transpose_chunks(d * (G * F), G * F // LANES)
        for k in range(1, G):
            norm_copy(d, k).start()
        a[rows(d, F), rows(c, T)] = nt[rows(d * G + c, F), :]
        if n == 0:
            for k in (1, 2):
                cot_copy(k).wait_recv()
                cot_pass(k).start()
            w_wait(1)
            if O > 2:
                w_start(2)
    for k in range(1, R):
        frag_copy(k).start()

    def sum_copy(d):
        side = jnp.where(z < d, 0, 1)
        return remote(
            out_buf.at[d], in_buf.at[side, d], sum_s.at[d], sum_r.at[side, d],
            at(r, jnp.where(z < d, z + 1, z - 1), c),
        )

    def sum_wait(side, d):
        where = in_buf.at[side, d]
        remote(where, where, sum_s.at[d], sum_r.at[side, d], at(r, z, plane[1])).wait_recv()

    def pass_on(d):
        between = jnp.logical_and(d != z, jnp.logical_and(z > 0, z < O - 1))

        @pl.when(between)
        def _():
            side = jnp.where(z < d, 0, 1)
            sum_wait(side, d)
            out_buf[d] = (part[d] + in_buf[side, d].astype(jnp.float32)).astype(jnp.bfloat16)
            sum_copy(d).start()

    tile = min(512, KV)
    for n in range(O):
        d = order(n)
        if n and n + 1 < O:
            w_wait(n + 1)
            if n + 2 < O:
                w_start(n + 2)
        if n == 0:
            for copy in mine:
                copy.wait()
            for k in (1, 2):
                cot_passed(k).wait_recv()
        for k in range(1, G):
            norm_copy(d, k).wait_recv()
        for m in range(KV // tile):
            cols = pl.ds(m * tile, tile)
            part[d, :, cols] = jnp.dot(a[rows(d, F), :], cots[:, cols], preferred_element_type=jnp.float32)
        first = jnp.logical_or(jnp.logical_and(z == 0, d > 0), jnp.logical_and(z == O - 1, d < O - 1))

        @pl.when(first)
        def _(d=d):
            out_buf[d] = part[d].astype(jnp.bfloat16)
            sum_copy(d).start()

        if n == O - 2:
            pass_on(order(0))

    top, bottom = pl.ds(0, half), pl.ds(half, half)

    def key_term(k, put):
        tokens = rows(plane[k], T)
        for m in range(KV // tile):
            cols = pl.ds(m * tile, tile)
            put(cols, lax.dot_general(
                a[:, tokens], ws[:, cols], (((0,), (0,)), ((), ())), preferred_element_type=jnp.float32
            ))

    def key_copy(k, part_of, slot, target):
        return remote(
            key_out.at[k, part_of], key_in.at[k, part_of], key_s.at[slot], key_r.at[slot], at(r, z, target)
        )

    across = [key_copy(3, top, 0, plane[1]), key_copy(3, bottom, 1, plane[2])]
    plain = [key_copy(1, top, 2, plane[1]), key_copy(2, bottom, 3, plane[2])]
    summed = [key_copy(1, bottom, 4, plane[1]), key_copy(2, top, 5, plane[2])]

    def put_across(cols, term):
        key_out[3, :, cols] = term.astype(jnp.bfloat16)

    key_term(3, put_across)
    for copy in across:
        copy.start()

    def put_x(cols, term):
        key_out[1, top, cols] = term[:half].astype(jnp.bfloat16)
        key_add[0, :, cols] = term[half:]

    key_term(1, put_x)
    plain[0].start()

    def put_y(cols, term):
        key_out[2, bottom, cols] = term[half:].astype(jnp.bfloat16)
        key_add[1, :, cols] = term[:half]

    key_term(2, put_y)
    plain[1].start()

    def put_own(cols, term):
        key_own[:, cols] = term

    key_term(0, put_own)
    across[1].wait_recv()
    key_out[1, bottom, :] = (key_add[0] + key_in[3, bottom, :].astype(jnp.float32)).astype(jnp.bfloat16)
    summed[0].start()
    across[0].wait_recv()
    key_out[2, top, :] = (key_add[1] + key_in[3, top, :].astype(jnp.float32)).astype(jnp.bfloat16)
    summed[1].start()

    for n in range(1, O):
        pass_on(order(n))

    grad_ref[...] = part[z]

    @pl.when(has_left)
    def _():
        sum_wait(0, z)
        grad_ref[...] += in_buf[0, z].astype(jnp.float32)

    @pl.when(has_right)
    def _():
        sum_wait(1, z)
        grad_ref[...] += in_buf[1, z].astype(jnp.float32)

    grad_ref[...] = grad_ref[...] * scale

    for copy in plain + summed:
        copy.wait_recv()
    total = key_own[...] + key_in[1].astype(jnp.float32) + key_in[2].astype(jnp.float32)
    keys_ref[...] = (total * scale).astype(jnp.bfloat16)

    for k in range(1, R):
        frag_copy(k).wait()
    for copy in across + plain + summed:
        copy.wait_send()
    for k in (1, 2):
        cot_copy(k).wait_send()
        cot_pass(k).wait_send()
    for d in range(O):
        for k in range(1, G):
            norm_copy(d, k).wait_send()

        @pl.when(z != d)
        def _(d=d):
            sum_copy(d).wait_send()
    for hop in range(1, O):
        for side in range(2):
            @pl.when(w_sends(side, hop))
            def _(side=side, hop=hop):
                w_copy(side, hop).wait_send()


def body(layer_index, inputs, norm_gain, cotangent, local_fragment, global_fragment, momentum):
    R, S = lax.axis_size("replica"), lax.axis_size("fsdp")
    G = INNER
    O = S // G
    T, D = inputs.shape
    KV = cotangent.shape[1]
    F = D // S
    own = local_fragment[0]
    bf16, f32 = jnp.bfloat16, jnp.float32
    vmem, anywhere = pl.BlockSpec(memory_space=pltpu.VMEM), pl.BlockSpec(memory_space=pl.ANY)
    dma = pltpu.SemaphoreType.DMA
    keys_block, grad, fragments = pl.pallas_call(
        functools.partial(kernel, R, G, O),
        out_shape=(
            jax.ShapeDtypeStruct((T, KV), bf16),
            jax.ShapeDtypeStruct((F, KV), f32),
            jax.ShapeDtypeStruct((R,) + own.shape, bf16),
        ),
        in_specs=[pl.BlockSpec(memory_space=pltpu.SMEM), anywhere, vmem, vmem, anywhere],
        out_specs=(vmem, vmem, anywhere),
        scratch_shapes=[
            pltpu.VMEM((T, D), bf16),
            pltpu.VMEM(own.shape, bf16),
            pltpu.VMEM((T, LANES), f32),
            pltpu.VMEM((D, T), bf16),
            pltpu.VMEM((O * F, G * T), bf16),
            pltpu.VMEM((G * T, KV), bf16),
            pltpu.VMEM((O * F, KV), bf16),
            pltpu.VMEM((O, F, KV), f32),
            pltpu.VMEM((O, F, KV), bf16),
            pltpu.VMEM((2, O, F, KV), bf16),
            pltpu.VMEM((T, KV), f32),
            pltpu.VMEM((2, T // 2, KV), f32),
            pltpu.VMEM((G, T, KV), bf16),
            pltpu.VMEM((G, T, KV), bf16),
            dma((4,)), dma((R,)), dma((R,)), dma((5,)), dma((5,)),
            dma((2, O)), dma((2, O)), dma((O, G)), dma((O, G)),
            dma((6,)), dma((6,)), dma((O,)), dma((2, O)),
        ],
        compiler_params=pltpu.CompilerParams(
            collective_id=0, has_side_effects=True, vmem_limit_bytes=56 * 1024 * 1024
        ),
        cost_estimate=pl.CostEstimate(flops=4 * T * D * KV, bytes_accessed=16 * 1024 * 1024, transcendentals=T),
    )(layer_index, inputs, norm_gain, cotangent, own)
    weight_grad = grad[None]
    total = global_fragment - fragments[0].astype(f32)
    for k in range(1, R):
        total = total + (global_fragment - fragments[k].astype(f32))
    average = total / R
    new_momentum = 0.9 * momentum + average
    new_global = global_fragment - 0.7 * (average + 0.9 * new_momentum)
    return (keys_block, weight_grad, new_global, new_momentum)


def solution(mesh):
    placed = (
        P("replica"),
        P(("replica", "fsdp"), None),
        P(),
        P(("replica", "fsdp"), None),
        P("replica", None, "fsdp", None),
        P(None, "fsdp", None),
        P(None, "fsdp", None),
    )
    return jax.shard_map(
        body,
        mesh=mesh,
        in_specs=placed,
        out_specs=(
            P(("replica", "fsdp"), None),
            P("replica", "fsdp", None),
            P(None, "fsdp", None),
            P(None, "fsdp", None),
        ),
        check_vma=False,
    )
```

```python
import functools

import jax
import jax.numpy as jnp
from jax import lax
from jax.experimental import pallas as pl
from jax.experimental.pallas import tpu as pltpu
from jax.sharding import PartitionSpec as P

INNER = 4
LANES = 128


def kernel(
    R, G, O, pick_ref, x_hbm, gain_ref, cot_ref, frag_hbm, keys_ref, grad_ref, frag_out,
    x_ref, frag_in, inv, nt, a, cots, ws, part, out_buf, in_buf, key_own, key_add, key_out, key_in,
    local_sem, frag_s, frag_r, cot_s, cot_r, w_s, w_r, norm_s, norm_r, key_s, key_r, sum_s, sum_r,
):
    T, D = x_ref.shape
    KV = cot_ref.shape[1]
    F = D // (G * O)
    scale = float(D) ** (-0.5)
    r = lax.axis_index("replica")
    i = lax.axis_index("fsdp")
    z, c = i // G, i % G
    cx, cy = c % 2, c // 2
    plane = [c, cy * 2 + 1 - cx, (1 - cy) * 2 + cx, 3 - c]

    def at(replica, outer, inner):
        return {"replica": replica, "fsdp": outer * G + inner}

    def remote(src, dst, send, recv, target):
        return pltpu.make_async_remote_copy(
            src_ref=src, dst_ref=dst, send_sem=send, recv_sem=recv,
            device_id=target, device_id_type=pl.DeviceIdType.MESH,
        )

    def rows(block, size):
        return pl.ds(pl.multiple_of(block * size, size), size)

    load_x = pltpu.make_async_copy(x_hbm, x_ref, local_sem.at[2])
    load_frag = pltpu.make_async_copy(frag_hbm, frag_in, local_sem.at[3])
    load_frag.start()
    load_x.start()

    barrier = pltpu.get_barrier_semaphore()

    def greet(target):
        pl.semaphore_signal(barrier, inc=1, device_id=target, device_id_type=pl.DeviceIdType.MESH)

    for k in range(1, G):
        greet(at(r, z, plane[k]))
    for k in range(1, R):
        greet(at((r + k) % R, z, c))
    has_left, has_right = z > 0, z < O - 1

    @pl.when(has_left)
    def _():
        greet(at(r, z - 1, c))

    @pl.when(has_right)
    def _():
        greet(at(r, z + 1, c))

    pl.semaphore_wait(barrier, G - 1 + R - 1 + jnp.where(has_left, 1, 0) + jnp.where(has_right, 1, 0))

    half = T // 2

    def cot_copy(k):
        return remote(cot_ref, cots.at[rows(c, T)], cot_s.at[k], cot_r.at[k], at(r, z, plane[k]))

    def cot_pass(k):
        where = cots.at[pl.ds(pl.multiple_of(plane[k] * T + (k - 1) * half, half), half)]
        return remote(where, where, cot_s.at[2 + k], cot_r.at[2 + k], at(r, z, plane[3 - k]))

    def cot_passed(k):
        where = cots.at[pl.ds(pl.multiple_of(plane[3] * T + (2 - k) * half, half), half)]
        return remote(where, where, cot_s.at[5 - k], cot_r.at[5 - k], at(r, z, plane[k]))

    def frag_copy(k):
        return remote(frag_in, frag_out.at[r], frag_s.at[k], frag_r.at[k], at((r + k) % R, z, c))

    def w_copy(side, hop):
        block = z - (hop - 1) if side == 0 else z + (hop - 1)
        where = ws.at[rows(block, F)]
        return remote(
            where, where, w_s.at[side, hop], w_r.at[side, hop],
            at(r, z + 1 if side == 0 else z - 1, c),
        )

    def w_sends(side, hop):
        if side == 0:
            return jnp.logical_and(z >= hop - 1, z < O - 1)
        return jnp.logical_and(z + hop - 1 <= O - 1, z > 0)

    def w_comes(side, hop):
        return z >= hop if side == 0 else z + hop <= O - 1

    def w_start(hop):
        for side in range(2):
            @pl.when(w_sends(side, hop))
            def _(side=side):
                w_copy(side, hop).start()

    def w_wait(hop):
        for side in range(2):
            @pl.when(w_comes(side, hop))
            def _(side=side):
                block = z - hop if side == 0 else z + hop
                where = ws.at[rows(block, F)]
                remote(where, where, w_s.at[side, hop], w_r.at[side, hop], at(r, z, plane[1])).wait_recv()

    for k in (1, 2):
        cot_copy(k).start()
    load_frag.wait()
    ws[rows(z, F), :] = frag_in[pick_ref[0]]
    w_start(1)
    mine = [
        pltpu.make_async_copy(cot_ref, cots.at[rows(c, T)], local_sem.at[0]),
        pltpu.make_async_copy(frag_in, frag_out.at[r], local_sem.at[1]),
    ]
    for copy in mine:
        copy.start()

    load_x.wait()
    step = 16

    @pl.loop(0, T // step)
    def _(t):
        here = pl.ds(pl.multiple_of(t * step, step), step)
        values = x_ref[here, :].astype(jnp.float32)
        stats = jnp.mean(values * values, axis=1, keepdims=True)
        inv[here, :] = jnp.broadcast_to(lax.rsqrt(stats + 1e-06), (step, LANES))

    def transpose_chunks(start, count):
        @pl.loop(0, count)
        def _(j):
            here = pl.ds(pl.multiple_of(start + j * LANES, LANES), LANES)
            normed = x_ref[:, here].astype(jnp.float32) * inv[...] * gain_ref[here][None, :]
            nt[here, :] = normed.T.astype(jnp.bfloat16)

    def order(k):
        far = O - 1 - k // 2 if k % 2 == 0 else k // 2
        return jnp.where(z < O // 2, far, O - 1 - far)

    def norm_copy(d, k):
        peer = plane[k]
        return remote(
            nt.at[rows(d * G + peer, F)],
            a.at[rows(d, F), rows(c, T)],
            norm_s.at[d, k], norm_r.at[d, k], at(r, z, peer),
        )

    whole = (G * F) % LANES != 0
    if whole:
        transpose_chunks(0, D // LANES)
    for n in range(O):
        d = order(n)
        if not whole:
            transpose_chunks(d * (G * F), G * F // LANES)
        for k in range(1, G):
            norm_copy(d, k).start()
        a[rows(d, F), rows(c, T)] = nt[rows(d * G + c, F), :]
        if n == 0:
            for k in (1, 2):
                cot_copy(k).wait_recv()
                cot_pass(k).start()
            w_wait(1)
            if O > 2:
                w_start(2)
    for k in range(1, R):
        frag_copy(k).start()

    tile = KV // 2
    halves = [pl.ds(m * tile, tile) for m in range(2)]

    def sum_copy(d, m):
        side = jnp.where(z < d, 0, 1)
        return remote(
            out_buf.at[d, :, halves[m]], in_buf.at[side, d, :, halves[m]], sum_s.at[d, m], sum_r.at[side, d, m],
            at(r, jnp.where(z < d, z + 1, z - 1), c),
        )

    def sum_wait(side, d, m):
        where = in_buf.at[side, d, :, halves[m]]
        remote(where, where, sum_s.at[d, m], sum_r.at[side, d, m], at(r, z, plane[1])).wait_recv()

    def pass_on(d):
        between = jnp.logical_and(d != z, jnp.logical_and(z > 0, z < O - 1))

        @pl.when(between)
        def _():
            side = jnp.where(z < d, 0, 1)
            for m, cols in enumerate(halves):
                sum_wait(side, d, m)
                got = in_buf[side, d, :, cols].astype(jnp.float32)
                out_buf[d, :, cols] = (part[d, :, cols] + got).astype(jnp.bfloat16)
                sum_copy(d, m).start()

    for n in range(O):
        d = order(n)
        if n and n + 1 < O:
            w_wait(n + 1)
            if n + 2 < O:
                w_start(n + 2)
        if n == 0:
            for copy in mine:
                copy.wait()
            for k in (1, 2):
                cot_passed(k).wait_recv()
        for k in range(1, G):
            norm_copy(d, k).wait_recv()
        first = jnp.logical_or(jnp.logical_and(z == 0, d > 0), jnp.logical_and(z == O - 1, d < O - 1))
        for m, cols in enumerate(halves):
            part[d, :, cols] = jnp.dot(a[rows(d, F), :], cots[:, cols], preferred_element_type=jnp.float32)

            @pl.when(first)
            def _(d=d, m=m, cols=cols):
                out_buf[d, :, cols] = part[d, :, cols].astype(jnp.bfloat16)
                sum_copy(d, m).start()

        if n == O - 2:
            pass_on(order(0))

    top, bottom = pl.ds(0, half), pl.ds(half, half)

    def key_term(k, put):
        tokens = rows(plane[k], T)
        for m in range(KV // tile):
            cols = pl.ds(m * tile, tile)
            put(cols, lax.dot_general(
                a[:, tokens], ws[:, cols], (((0,), (0,)), ((), ())), preferred_element_type=jnp.float32
            ))

    def key_copy(k, part_of, slot, target):
        return remote(
            key_out.at[k, part_of], key_in.at[k, part_of], key_s.at[slot], key_r.at[slot], at(r, z, target)
        )

    across = [key_copy(3, top, 0, plane[1]), key_copy(3, bottom, 1, plane[2])]
    plain = [key_copy(1, top, 2, plane[1]), key_copy(2, bottom, 3, plane[2])]
    summed = [key_copy(1, bottom, 4, plane[1]), key_copy(2, top, 5, plane[2])]

    def put_across(cols, term):
        key_out[3, :, cols] = term.astype(jnp.bfloat16)

    key_term(3, put_across)
    for copy in across:
        copy.start()

    def put_x(cols, term):
        key_out[1, top, cols] = term[:half].astype(jnp.bfloat16)
        key_add[0, :, cols] = term[half:]

    key_term(1, put_x)
    plain[0].start()

    def put_y(cols, term):
        key_out[2, bottom, cols] = term[half:].astype(jnp.bfloat16)
        key_add[1, :, cols] = term[:half]

    key_term(2, put_y)
    plain[1].start()

    def put_own(cols, term):
        key_own[:, cols] = term

    key_term(0, put_own)
    across[1].wait_recv()
    key_out[1, bottom, :] = (key_add[0] + key_in[3, bottom, :].astype(jnp.float32)).astype(jnp.bfloat16)
    summed[0].start()
    across[0].wait_recv()
    key_out[2, top, :] = (key_add[1] + key_in[3, top, :].astype(jnp.float32)).astype(jnp.bfloat16)
    summed[1].start()

    for n in range(1, O):
        pass_on(order(n))

    grad_ref[...] = part[z]

    @pl.when(has_left)
    def _():
        for m in range(2):
            sum_wait(0, z, m)
        grad_ref[...] += in_buf[0, z].astype(jnp.float32)

    @pl.when(has_right)
    def _():
        for m in range(2):
            sum_wait(1, z, m)
        grad_ref[...] += in_buf[1, z].astype(jnp.float32)

    grad_ref[...] = grad_ref[...] * scale

    for copy in plain + summed:
        copy.wait_recv()
    total = key_own[...] + key_in[1].astype(jnp.float32) + key_in[2].astype(jnp.float32)
    keys_ref[...] = (total * scale).astype(jnp.bfloat16)

    for k in range(1, R):
        frag_copy(k).wait()
    for copy in across + plain + summed:
        copy.wait_send()
    for k in (1, 2):
        cot_copy(k).wait_send()
        cot_pass(k).wait_send()
    for d in range(O):
        for k in range(1, G):
            norm_copy(d, k).wait_send()

        @pl.when(z != d)
        def _(d=d):
            for m in range(2):
                sum_copy(d, m).wait_send()
    for hop in range(1, O):
        for side in range(2):
            @pl.when(w_sends(side, hop))
            def _(side=side, hop=hop):
                w_copy(side, hop).wait_send()


def body(layer_index, inputs, norm_gain, cotangent, local_fragment, global_fragment, momentum):
    R, S = lax.axis_size("replica"), lax.axis_size("fsdp")
    G = INNER
    O = S // G
    T, D = inputs.shape
    KV = cotangent.shape[1]
    F = D // S
    own = local_fragment[0]
    bf16, f32 = jnp.bfloat16, jnp.float32
    vmem, anywhere = pl.BlockSpec(memory_space=pltpu.VMEM), pl.BlockSpec(memory_space=pl.ANY)
    dma = pltpu.SemaphoreType.DMA
    keys_block, grad, fragments = pl.pallas_call(
        functools.partial(kernel, R, G, O),
        out_shape=(
            jax.ShapeDtypeStruct((T, KV), bf16),
            jax.ShapeDtypeStruct((F, KV), f32),
            jax.ShapeDtypeStruct((R,) + own.shape, bf16),
        ),
        in_specs=[pl.BlockSpec(memory_space=pltpu.SMEM), anywhere, vmem, vmem, anywhere],
        out_specs=(vmem, vmem, anywhere),
        scratch_shapes=[
            pltpu.VMEM((T, D), bf16),
            pltpu.VMEM(own.shape, bf16),
            pltpu.VMEM((T, LANES), f32),
            pltpu.VMEM((D, T), bf16),
            pltpu.VMEM((O * F, G * T), bf16),
            pltpu.VMEM((G * T, KV), bf16),
            pltpu.VMEM((O * F, KV), bf16),
            pltpu.VMEM((O, F, KV), f32),
            pltpu.VMEM((O, F, KV), bf16),
            pltpu.VMEM((2, O, F, KV), bf16),
            pltpu.VMEM((T, KV), f32),
            pltpu.VMEM((2, T // 2, KV), f32),
            pltpu.VMEM((G, T, KV), bf16),
            pltpu.VMEM((G, T, KV), bf16),
            dma((4,)), dma((R,)), dma((R,)), dma((5,)), dma((5,)),
            dma((2, O)), dma((2, O)), dma((O, G)), dma((O, G)),
            dma((6,)), dma((6,)), dma((O, 2)), dma((2, O, 2)),
        ],
        compiler_params=pltpu.CompilerParams(
            collective_id=0, has_side_effects=True, vmem_limit_bytes=40 * 1024 * 1024
        ),
        cost_estimate=pl.CostEstimate(flops=4 * T * D * KV, bytes_accessed=16 * 1024 * 1024, transcendentals=T),
    )(layer_index, inputs, norm_gain, cotangent, own)
    weight_grad = grad[None]
    total = global_fragment - fragments[0].astype(f32)
    for k in range(1, R):
        total = total + (global_fragment - fragments[k].astype(f32))
    average = total / R
    new_momentum = 0.9 * momentum + average
    new_global = global_fragment - 0.7 * (average + 0.9 * new_momentum)
    return (keys_block, weight_grad, new_global, new_momentum)


def solution(mesh):
    placed = (
        P("replica"),
        P(("replica", "fsdp"), None),
        P(),
        P(("replica", "fsdp"), None),
        P("replica", None, "fsdp", None),
        P(None, "fsdp", None),
        P(None, "fsdp", None),
    )
    return jax.shard_map(
        body,
        mesh=mesh,
        in_specs=placed,
        out_specs=(
            P(("replica", "fsdp"), None),
            P("replica", "fsdp", None),
            P(None, "fsdp", None),
            P(None, "fsdp", None),
        ),
        check_vma=False,
    )
```

```python
import functools

import jax
import jax.numpy as jnp
from jax import lax
from jax.experimental import pallas as pl
from jax.experimental.pallas import tpu as pltpu
from jax.sharding import PartitionSpec as P

INNER = 4
LANES = 128


def kernel(
    R, G, O, pick_ref, x_hbm, gain_ref, cot_ref, frag_hbm, keys_ref, grad_ref, frag_out,
    x_ref, frag_in, inv, nt, a, cots, ws, part, out_buf, in_buf, key_own, key_add, key_out, key_in,
    local_sem, frag_s, frag_r, cot_s, cot_r, w_s, w_r, norm_s, norm_r, key_s, key_r, sum_s, sum_r,
):
    T, D = x_ref.shape
    KV = cot_ref.shape[1]
    F = D // (G * O)
    scale = float(D) ** (-0.5)
    r = lax.axis_index("replica")
    i = lax.axis_index("fsdp")
    z, c = i // G, i % G
    cx, cy = c % 2, c // 2
    plane = [c, cy * 2 + 1 - cx, (1 - cy) * 2 + cx, 3 - c]

    def at(replica, outer, inner):
        return {"replica": replica, "fsdp": outer * G + inner}

    def remote(src, dst, send, recv, target):
        return pltpu.make_async_remote_copy(
            src_ref=src, dst_ref=dst, send_sem=send, recv_sem=recv,
            device_id=target, device_id_type=pl.DeviceIdType.MESH,
        )

    def rows(block, size):
        return pl.ds(pl.multiple_of(block * size, size), size)

    load_x = pltpu.make_async_copy(x_hbm, x_ref, local_sem.at[2])
    load_frag = pltpu.make_async_copy(frag_hbm, frag_in, local_sem.at[3])
    load_frag.start()
    load_x.start()

    barrier = pltpu.get_barrier_semaphore()

    def greet(target):
        pl.semaphore_signal(barrier, inc=1, device_id=target, device_id_type=pl.DeviceIdType.MESH)

    for k in range(1, G):
        greet(at(r, z, plane[k]))
    for k in range(1, R):
        greet(at((r + k) % R, z, c))
    has_left, has_right = z > 0, z < O - 1

    @pl.when(has_left)
    def _():
        greet(at(r, z - 1, c))

    @pl.when(has_right)
    def _():
        greet(at(r, z + 1, c))

    pl.semaphore_wait(barrier, G - 1 + R - 1 + jnp.where(has_left, 1, 0) + jnp.where(has_right, 1, 0))

    half = T // 2

    def cot_copy(k):
        return remote(cot_ref, cots.at[rows(c, T)], cot_s.at[k], cot_r.at[k], at(r, z, plane[k]))

    def cot_pass(k):
        where = cots.at[pl.ds(pl.multiple_of(plane[k] * T + (k - 1) * half, half), half)]
        return remote(where, where, cot_s.at[2 + k], cot_r.at[2 + k], at(r, z, plane[3 - k]))

    def cot_passed(k):
        where = cots.at[pl.ds(pl.multiple_of(plane[3] * T + (2 - k) * half, half), half)]
        return remote(where, where, cot_s.at[5 - k], cot_r.at[5 - k], at(r, z, plane[k]))

    def frag_copy(k):
        return remote(frag_in, frag_out.at[r], frag_s.at[k], frag_r.at[k], at((r + k) % R, z, c))

    def w_copy(side, hop):
        block = z - (hop - 1) if side == 0 else z + (hop - 1)
        where = ws.at[rows(block, F)]
        return remote(
            where, where, w_s.at[side, hop], w_r.at[side, hop],
            at(r, z + 1 if side == 0 else z - 1, c),
        )

    def w_sends(side, hop):
        if side == 0:
            return jnp.logical_and(z >= hop - 1, z < O - 1)
        return jnp.logical_and(z + hop - 1 <= O - 1, z > 0)

    def w_comes(side, hop):
        return z >= hop if side == 0 else z + hop <= O - 1

    def w_start(hop):
        for side in range(2):
            @pl.when(w_sends(side, hop))
            def _(side=side):
                w_copy(side, hop).start()

    def w_wait(hop):
        for side in range(2):
            @pl.when(w_comes(side, hop))
            def _(side=side):
                block = z - hop if side == 0 else z + hop
                where = ws.at[rows(block, F)]
                remote(where, where, w_s.at[side, hop], w_r.at[side, hop], at(r, z, plane[1])).wait_recv()

    for k in (1, 2):
        cot_copy(k).start()
    load_frag.wait()
    ws[rows(z, F), :] = frag_in[pick_ref[0]]
    w_start(1)
    mine = [
        pltpu.make_async_copy(cot_ref, cots.at[rows(c, T)], local_sem.at[0]),
        pltpu.make_async_copy(frag_in, frag_out.at[r], local_sem.at[1]),
    ]
    for copy in mine:
        copy.start()

    load_x.wait()
    step = 16

    @pl.loop(0, T // step)
    def _(t):
        here = pl.ds(pl.multiple_of(t * step, step), step)
        values = x_ref[here, :].astype(jnp.float32)
        stats = jnp.mean(values * values, axis=1, keepdims=True)
        inv[here, :] = jnp.broadcast_to(lax.rsqrt(stats + 1e-06), (step, LANES))

    def transpose_chunks(start, count):
        @pl.loop(0, count)
        def _(j):
            here = pl.ds(pl.multiple_of(start + j * LANES, LANES), LANES)
            normed = x_ref[:, here].astype(jnp.float32) * inv[...] * gain_ref[here][None, :]
            nt[here, :] = normed.T.astype(jnp.bfloat16)

    def order(k):
        far = O - 1 - k // 2 if k % 2 == 0 else k // 2
        return jnp.where(z < O // 2, far, O - 1 - far)

    def norm_copy(d, k):
        peer = plane[k]
        return remote(
            nt.at[rows(d * G + peer, F)],
            a.at[rows(d, F), rows(c, T)],
            norm_s.at[d, k], norm_r.at[d, k], at(r, z, peer),
        )

    whole = (G * F) % LANES != 0
    if whole:
        transpose_chunks(0, D // LANES)
    for n in range(O):
        d = order(n)
        if not whole:
            transpose_chunks(d * (G * F), G * F // LANES)
        for k in range(1, G):
            norm_copy(d, k).start()
        a[rows(d, F), rows(c, T)] = nt[rows(d * G + c, F), :]
        if n == 0:
            for k in (1, 2):
                cot_copy(k).wait_recv()
                cot_pass(k).start()
            w_wait(1)
            if O > 2:
                w_start(2)
    for k in range(1, R):
        frag_copy(k).start()

    tile = KV // 2
    halves = [pl.ds(m * tile, tile) for m in range(2)]

    def sum_copy(d, m):
        side = jnp.where(z < d, 0, 1)
        return remote(
            out_buf.at[d, :, halves[m]], in_buf.at[side, d, :, halves[m]], sum_s.at[d, m], sum_r.at[side, d, m],
            at(r, jnp.where(z < d, z + 1, z - 1), c),
        )

    def sum_wait(side, d, m):
        where = in_buf.at[side, d, :, halves[m]]
        remote(where, where, sum_s.at[d, m], sum_r.at[side, d, m], at(r, z, plane[1])).wait_recv()

    def pass_on(d):
        between = jnp.logical_and(d != z, jnp.logical_and(z > 0, z < O - 1))

        @pl.when(between)
        def _():
            side = jnp.where(z < d, 0, 1)
            for m, cols in enumerate(halves):
                sum_wait(side, d, m)
                got = in_buf[side, d, :, cols].astype(jnp.float32)
                out_buf[d, :, cols] = (part[d, :, cols] + got).astype(jnp.bfloat16)
                sum_copy(d, m).start()

    for n in range(O):
        d = order(n)
        if n and n + 1 < O:
            w_wait(n + 1)
            if n + 2 < O:
                w_start(n + 2)
        if n == 0:
            for copy in mine:
                copy.wait()
            for k in (1, 2):
                cot_passed(k).wait_recv()
        for k in range(1, G):
            norm_copy(d, k).wait_recv()
        first = jnp.logical_or(jnp.logical_and(z == 0, d > 0), jnp.logical_and(z == O - 1, d < O - 1))
        for m, cols in enumerate(halves):
            part[d, :, cols] = jnp.dot(a[rows(d, F), :], cots[:, cols], preferred_element_type=jnp.float32)

            @pl.when(first)
            def _(d=d, m=m, cols=cols):
                out_buf[d, :, cols] = part[d, :, cols].astype(jnp.bfloat16)
                sum_copy(d, m).start()

        if n == O - 2:
            pass_on(order(0))

    top, bottom = pl.ds(0, half), pl.ds(half, half)

    def key_term(k, put):
        tokens = rows(plane[k], T)
        for m in range(KV // tile):
            cols = pl.ds(m * tile, tile)
            put(cols, lax.dot_general(
                a[:, tokens], ws[:, cols], (((0,), (0,)), ((), ())), preferred_element_type=jnp.float32
            ))

    def key_copy(k, part_of, slot, target):
        return remote(
            key_out.at[k, part_of], key_in.at[k, part_of], key_s.at[slot], key_r.at[slot], at(r, z, target)
        )

    across = [key_copy(3, top, 0, plane[1]), key_copy(3, bottom, 1, plane[2])]
    plain = [key_copy(1, top, 2, plane[1]), key_copy(2, bottom, 3, plane[2])]
    summed = [key_copy(1, bottom, 4, plane[1]), key_copy(2, top, 5, plane[2])]

    def put_across(cols, term):
        key_out[3, :, cols] = term.astype(jnp.bfloat16)

    key_term(3, put_across)
    for copy in across:
        copy.start()

    def put_x(cols, term):
        key_out[1, top, cols] = term[:half].astype(jnp.bfloat16)
        key_add[0, :, cols] = term[half:]

    key_term(1, put_x)
    plain[0].start()

    def put_y(cols, term):
        key_out[2, bottom, cols] = term[half:].astype(jnp.bfloat16)
        key_add[1, :, cols] = term[:half]

    key_term(2, put_y)
    plain[1].start()

    def put_own(cols, term):
        key_own[:, cols] = term

    key_term(0, put_own)
    across[1].wait_recv()
    key_out[1, bottom, :] = (key_add[0] + key_in[3, bottom, :].astype(jnp.float32)).astype(jnp.bfloat16)
    summed[0].start()
    across[0].wait_recv()
    key_out[2, top, :] = (key_add[1] + key_in[3, top, :].astype(jnp.float32)).astype(jnp.bfloat16)
    summed[1].start()

    for n in range(1, O):
        pass_on(order(n))

    grad_ref[...] = part[z]

    @pl.when(has_left)
    def _():
        for m in range(2):
            sum_wait(0, z, m)
        grad_ref[...] += in_buf[0, z].astype(jnp.float32)

    @pl.when(has_right)
    def _():
        for m in range(2):
            sum_wait(1, z, m)
        grad_ref[...] += in_buf[1, z].astype(jnp.float32)

    grad_ref[...] = grad_ref[...] * scale

    for copy in plain + summed:
        copy.wait_recv()
    total = key_own[...] + key_in[1].astype(jnp.float32) + key_in[2].astype(jnp.float32)
    keys_ref[...] = (total * scale).astype(jnp.bfloat16)

    for k in range(1, R):
        frag_copy(k).wait()
    for copy in across + plain + summed:
        copy.wait_send()
    for k in (1, 2):
        cot_copy(k).wait_send()
        cot_pass(k).wait_send()
    for d in range(O):
        for k in range(1, G):
            norm_copy(d, k).wait_send()

        @pl.when(z != d)
        def _(d=d):
            for m in range(2):
                sum_copy(d, m).wait_send()
    for hop in range(1, O):
        for side in range(2):
            @pl.when(w_sends(side, hop))
            def _(side=side, hop=hop):
                w_copy(side, hop).wait_send()


def body(layer_index, inputs, norm_gain, cotangent, local_fragment, global_fragment, momentum):
    R, S = lax.axis_size("replica"), lax.axis_size("fsdp")
    G = INNER
    O = S // G
    T, D = inputs.shape
    KV = cotangent.shape[1]
    F = D // S
    own = local_fragment[0]
    bf16, f32 = jnp.bfloat16, jnp.float32
    vmem, anywhere = pl.BlockSpec(memory_space=pltpu.VMEM), pl.BlockSpec(memory_space=pl.ANY)
    dma = pltpu.SemaphoreType.DMA
    keys_block, grad, fragments = pl.pallas_call(
        functools.partial(kernel, R, G, O),
        out_shape=(
            jax.ShapeDtypeStruct((T, KV), bf16),
            jax.ShapeDtypeStruct((F, KV), f32),
            jax.ShapeDtypeStruct((R,) + own.shape, bf16),
        ),
        in_specs=[pl.BlockSpec(memory_space=pltpu.SMEM), anywhere, vmem, vmem, anywhere],
        out_specs=(vmem, vmem, anywhere),
        scratch_shapes=[
            pltpu.VMEM((T, D), bf16),
            pltpu.VMEM(own.shape, bf16),
            pltpu.VMEM((T, LANES), f32),
            pltpu.VMEM((D, T), bf16),
            pltpu.VMEM((O * F, G * T), bf16),
            pltpu.VMEM((G * T, KV), bf16),
            pltpu.VMEM((O * F, KV), bf16),
            pltpu.VMEM((O, F, KV), f32),
            pltpu.VMEM((O, F, KV), bf16),
            pltpu.VMEM((2, O, F, KV), bf16),
            pltpu.VMEM((T, KV), f32),
            pltpu.VMEM((2, T // 2, KV), f32),
            pltpu.VMEM((G, T, KV), bf16),
            pltpu.VMEM((G, T, KV), bf16),
            dma((4,)), dma((R,)), dma((R,)), dma((5,)), dma((5,)),
            dma((2, O)), dma((2, O)), dma((O, G)), dma((O, G)),
            dma((6,)), dma((6,)), dma((O, 2)), dma((2, O, 2)),
        ],
        compiler_params=pltpu.CompilerParams(
            collective_id=0, has_side_effects=True, vmem_limit_bytes=50 * 1024 * 1024
        ),
        cost_estimate=pl.CostEstimate(flops=4 * T * D * KV, bytes_accessed=16 * 1024 * 1024, transcendentals=T),
    )(layer_index, inputs, norm_gain, cotangent, own)
    weight_grad = grad[None]
    total = global_fragment - fragments[0].astype(f32)
    for k in range(1, R):
        total = total + (global_fragment - fragments[k].astype(f32))
    average = total / R
    new_momentum = 0.9 * momentum + average
    new_global = global_fragment - 0.7 * (average + 0.9 * new_momentum)
    return (keys_block, weight_grad, new_global, new_momentum)


def solution(mesh):
    placed = (
        P("replica"),
        P(("replica", "fsdp"), None),
        P(),
        P(("replica", "fsdp"), None),
        P("replica", None, "fsdp", None),
        P(None, "fsdp", None),
        P(None, "fsdp", None),
    )
    return jax.shard_map(
        body,
        mesh=mesh,
        in_specs=placed,
        out_specs=(
            P(("replica", "fsdp"), None),
            P("replica", "fsdp", None),
            P(None, "fsdp", None),
            P(None, "fsdp", None),
        ),
        check_vma=False,
    )
```
